32 devices in a mesh: row: 8 (over z, x), col: 4 (over y, core).
Axes of the slice: x: 2, y: 2, z: 4, core: 2. Of those that a mesh axis runs over, the one named last changes fastest.
Arguments:
- initial_estimate0: float32 [96, 128, 1024], P(None, 'row', 'col'), may hold values from 0.1 to 1
- clutter: float32 [128, 1024], P('row', 'col'), may hold values from 0 to 1.5
- counts: int32 [32, 96, 128], P(('row', 'col')), may hold values from 1 to 10000
- antenna_settings: float32 [32, 5, 128], P(('row', 'col')), as said below
- tile_block_list: int32 [8, 4, 32], P('row', 'col'), may hold values from 0 to 31, as said below
- tile_block_count: int32 [8, 4], P('row', 'col'), may hold values from 1 to 32
Outputs:
- estimate: float32 [96, 128, 1024], P(None, 'row', 'col')
The draws below stay inside these ranges and needn't reach their ends.
Inputs may be any that keep to these rules, and one draw needn't show every extreme that they name: `tile_block_list`: block b's owner group along row is b // 4; entry i of a tile's list is used only when i < tile_block_count, and unused entries hold 0; the listed blocks of one tile are distinct; every block is listed by some tile; one tile lists at most 4 blocks of one owner group, and the tiles of some column list 32 blocks each. `antenna_settings`: radii and gains are positive.
All inputs are finite; a program needn't handle non-finite values.
Results may differ from the reference program's by a relative error of at most 0.0003.
Values sent between devices are 32-bit elements; how exact they have to be, the bound alone decides.
A program may use at most 64 MiB of HBM per device.

```python
import math
import jax
import jax.numpy as jnp
from jax import lax

QUARTER_MAPS = 96
TR = 16
TC = 256
BLOCK_ANTENNAS = 128
TILE_BLOCK_LIMIT = 32
ITERS = 2
GR = 128
GC = 1024
ANTENNA_BLOCKS = 32
N_ROW = 8
N_COL = 4


def list_parts(key):
    base = jax.random.randint(jax.random.fold_in(key, 11), (N_ROW, N_COL), TILE_BLOCK_LIMIT // 4, TILE_BLOCK_LIMIT // 2 + 1)
    full_col = jax.random.randint(jax.random.fold_in(key, 12), (), 0, N_COL)
    columns = jnp.arange(N_COL, dtype=jnp.int32)[None, :]
    listed = jnp.where(columns == full_col, TILE_BLOCK_LIMIT, base).astype(jnp.int32)
    tile_index = jnp.arange(N_ROW, dtype=jnp.int32)[:, None] * N_COL + columns
    first = jnp.clip(tile_index - listed // 2, 0, N_ROW * N_COL - listed)
    slots = jnp.arange(TILE_BLOCK_LIMIT, dtype=jnp.int32)
    spatial = first[:, :, None] + slots[None, None, :]
    block_numbers = spatial % N_ROW * N_COL + spatial // N_ROW
    block_numbers = jnp.where(slots[None, None, :] < listed[:, :, None], block_numbers, 0)
    return (listed, block_numbers.astype(jnp.int32))


def draw_tile_block_list(key, part):
    return list_parts(jax.random.fold_in(key, 5))[1]


def draw_tile_block_count(key, part):
    return list_parts(jax.random.fold_in(key, 5))[0]


def draw_antenna_settings(key, part):
    blocks = jnp.arange(ANTENNA_BLOCKS, dtype=jnp.int32)
    spatial = blocks % N_COL * N_ROW + blocks // N_COL
    home_row = (spatial // N_COL).astype(jnp.float32)
    home_col = (spatial % N_COL).astype(jnp.float32)
    row_shift = jax.random.uniform(jax.random.fold_in(key, 21), (ANTENNA_BLOCKS, BLOCK_ANTENNAS), jnp.float32, -1.0, 2.0)
    column_shift = jax.random.uniform(jax.random.fold_in(key, 22), (ANTENNA_BLOCKS, BLOCK_ANTENNAS), jnp.float32, -0.5, 1.5)
    position_row = (home_row[:, None] + row_shift) * TR
    position_column = (home_col[:, None] + column_shift) * TC
    antenna_radius = jnp.exp(jax.random.uniform(jax.random.fold_in(key, 23), (ANTENNA_BLOCKS, BLOCK_ANTENNAS), jnp.float32, jnp.log(16.0), jnp.log(256.0)))
    antenna_gain = jnp.exp(jax.random.uniform(jax.random.fold_in(key, 24), (ANTENNA_BLOCKS, BLOCK_ANTENNAS), jnp.float32, jnp.log(0.5), jnp.log(2.0)))
    antenna_group = jax.random.uniform(jax.random.fold_in(key, 25), (ANTENNA_BLOCKS, BLOCK_ANTENNAS), jnp.float32, 0.5, 2.0)
    return jnp.stack([position_row, position_column, antenna_radius, antenna_gain, antenna_group], axis=1).astype(jnp.float32)


def plant(drawn, rng, smallest, high):
    place = [jax.random.randint(jax.random.fold_in(rng, axis), (), 0, length) for axis, length in enumerate(drawn.shape)]
    widest = drawn.shape.index(max(drawn.shape))
    beside = place[:widest] + [(place[widest] + 1) % drawn.shape[widest]] + place[widest + 1:]
    return drawn.at[tuple(place)].set(smallest).at[tuple(beside)].set(high)


def steps_of(rng, dims, cuts, smallest, high):
    gain, own = 1.0, jax.random.fold_in(rng, 6)
    for dim, shards_of in cuts:
        steps = jnp.exp(jax.random.uniform(jax.random.fold_in(own, dim), (shards_of,), jnp.float32, smallest / len(cuts), high / len(cuts)))
        gain = gain * jnp.repeat(steps, dims[dim] // shards_of).reshape([-1 if axis == dim else 1 for axis in range(len(dims))])
    return gain


def setup_inputs(seed: int = 0) -> dict:
    seeds = jax.random.split(jax.random.key(seed), 7)
    initial_estimate0 = jnp.clip(jnp.exp(math.log(1.0) - 2.3025851 * jax.random.uniform(seeds[0], (QUARTER_MAPS, GR, GC), jnp.float32) ** steps_of(seeds[0], (QUARTER_MAPS, GR, GC), ((1, 8), (2, 4)), -0.2, 0.2)), 0.1, 1.0)
    clutter = jnp.clip(1.5 * jax.random.uniform(seeds[1], (GR, GC), jnp.float32) ** steps_of(seeds[1], (GR, GC), ((0, 8), (1, 4)), -0.2, 0.2), 0.0, 1.5)
    counts = plant(jax.random.randint(seeds[2], (ANTENNA_BLOCKS, QUARTER_MAPS, BLOCK_ANTENNAS), 1, 10001), jax.random.fold_in(seeds[2], 1), 1, 10000).astype(jnp.int32)
    antenna_settings = draw_antenna_settings(jax.random.fold_in(seeds[6], 71), 0)
    tile_block_list = draw_tile_block_list(jax.random.fold_in(seeds[6], 71), 0)
    tile_block_count = draw_tile_block_count(jax.random.fold_in(seeds[6], 71), 0)
    return dict(initial_estimate0=initial_estimate0, clutter=clutter, counts=counts, antenna_settings=antenna_settings, tile_block_list=tile_block_list, tile_block_count=tile_block_count)


def coverage(settings_rows, terrain_loss, pixel_row, pixel_column):
    antenna_row = settings_rows[:, 0, :, None]
    antenna_column = settings_rows[:, 1, :, None]
    antenna_radius = settings_rows[:, 2, :, None]
    antenna_gain = settings_rows[:, 3, :, None]
    antenna_group = settings_rows[:, 4, :, None]
    row_distance = pixel_row[None, None, :] - antenna_row
    column_distance = pixel_column[None, None, :] - antenna_column
    return antenna_gain * jnp.exp(-antenna_group * terrain_loss[None, None, :]) / (1.0 + (row_distance * row_distance + column_distance * column_distance) / (antenna_radius * antenna_radius))


def tile_coverage(tile_index, clutter, antenna_settings, flattened_lists, flattened_counts):
    tile_row = tile_index // N_COL
    tile_col = tile_index % N_COL
    local_row = jnp.repeat(jnp.arange(TR, dtype=jnp.int32), TC)
    local_col = jnp.tile(jnp.arange(TC, dtype=jnp.int32), TR)
    pixel_row = (tile_row * TR + local_row).astype(jnp.float32) + 0.5
    pixel_column = (tile_col * TC + local_col).astype(jnp.float32) + 0.5
    terrain_loss = lax.dynamic_slice(clutter, ((tile_row * TR).astype(jnp.int32), (tile_col * TC).astype(jnp.int32)), (TR, TC)).reshape(TR * TC)
    block_numbers = flattened_lists[tile_index]
    slot_live = (jnp.arange(TILE_BLOCK_LIMIT, dtype=jnp.int32) < flattened_counts[tile_index]).astype(jnp.float32)
    settings_rows = antenna_settings[block_numbers]
    return coverage(settings_rows, terrain_loss, pixel_row, pixel_column) * slot_live[:, None, None]


def reference(initial_estimate0, clutter, counts, antenna_settings, tile_block_list, tile_block_count):
    tile_count = N_ROW * N_COL
    n_pixels = TR * TC
    est_tiles = initial_estimate0.reshape(QUARTER_MAPS, N_ROW, TR, N_COL, TC).transpose(1, 3, 0, 2, 4).reshape(tile_count, QUARTER_MAPS, n_pixels)
    flattened_lists = tile_block_list.reshape(tile_count, TILE_BLOCK_LIMIT)
    flattened_counts = tile_block_count.reshape(tile_count)
    tile_ids = jnp.arange(tile_count, dtype=jnp.int32)
    highest = lax.Precision.HIGHEST

    def forward_first(args):
        tile_index, estimate = args
        coverage_value = tile_coverage(tile_index, clutter, antenna_settings, flattened_lists, flattened_counts)
        partial_value = jnp.einsum('tp,sap->sta', estimate, coverage_value, precision=highest)
        return partial_value, jnp.sum(coverage_value, axis=(0, 1))

    def forward(args):
        tile_index, estimate = args
        coverage_value = tile_coverage(tile_index, clutter, antenna_settings, flattened_lists, flattened_counts)
        return jnp.einsum('tp,sap->sta', estimate, coverage_value, precision=highest)

    sensitivity = None
    for sweep in range(ITERS):
        if sweep == 0:
            partial_sums, sensitivity = lax.map(forward_first, (tile_ids, est_tiles))
        else:
            partial_sums = lax.map(forward, (tile_ids, est_tiles))
        projected_counts = jnp.zeros((ANTENNA_BLOCKS, QUARTER_MAPS, BLOCK_ANTENNAS), jnp.float32).at[flattened_lists.reshape(-1)].add(partial_sums.reshape(tile_count * TILE_BLOCK_LIMIT, QUARTER_MAPS, BLOCK_ANTENNAS))
        ratios = counts.astype(jnp.float32) / projected_counts

        def backward(args):
            tile_index, estimate, sens_tile = args
            coverage_value = tile_coverage(tile_index, clutter, antenna_settings, flattened_lists, flattened_counts)
            picked = ratios[flattened_lists[tile_index]]
            backsum = jnp.einsum('sta,sap->tp', picked, coverage_value, precision=highest)
            return estimate * backsum / sens_tile[None, :]

        est_tiles = lax.map(backward, (tile_ids, est_tiles, sensitivity))
    return est_tiles.reshape(N_ROW, N_COL, QUARTER_MAPS, TR, TC).transpose(2, 0, 3, 1, 4).reshape(QUARTER_MAPS, GR, GC)
```

```python
import jax
import jax.numpy as jnp
from jax import lax
from jax.experimental import pallas as pl
from jax.experimental.pallas import tpu as pltpu
from jax.sharding import PartitionSpec as P

ITERS = 2
GROUP = 4
CHUNK = 512
LOG2E = 1.4426950408889634
NT = (((1,), (1,)), ((), ()))
VMEM = 50 << 20


def cover_kernel(
    meta, settings, clutter, estimate, cover, partial, column_term, slope, shift, inverse, total
):
    slots, rows, columns = meta.shape[0] - 3, clutter.shape[0], clutter.shape[2]
    antennas = settings.shape[2]
    step = pl.program_id(0)
    wide = (antennas, 128)

    @pl.when(step == 0)
    def _():
        partial[...] = jnp.zeros_like(partial)

    row_start = meta[slots + 1].astype(jnp.float32) + 0.5
    column_start = meta[slots + 2].astype(jnp.float32) + 0.5
    lanes = lax.broadcasted_iota(jnp.int32, wide, 1).astype(jnp.float32)
    for s in range(GROUP):
        here = slice(s * antennas, (s + 1) * antennas)
        record = jnp.transpose(settings[meta[step * GROUP + s]])
        inv = jnp.broadcast_to(1.0 / record[:, 2:3], wide)
        inverse[here, :] = inv
        shift[here, :] = (row_start - jnp.broadcast_to(record[:, 0:1], wide)) * inv
        slope[here, :] = jnp.broadcast_to(record[:, 4:5] * (-LOG2E), wide)
        position = jnp.broadcast_to(record[:, 1:2], wide)
        for h in range(columns // 128):
            d = (lanes + (column_start + h * 128.0) - position) * inv
            column_term[here, h * 128 : (h + 1) * 128] = 1.0 + d * d
    total[...] = jnp.zeros_like(total)

    def row(i, carry):
        base = pl.multiple_of(i * columns, columns)
        offset = i.astype(jnp.float32)
        for s in range(GROUP):
            here = slice(s * antennas, (s + 1) * antennas)
            d = shift[here, :] + offset * inverse[here, :]
            dd = d * d
            k = slope[here, :]
            for h in range(columns // 128):
                loss = clutter[i, :, h * 128 : (h + 1) * 128]
                c = jnp.exp2(k * loss) * pl.reciprocal(
                    dd + column_term[here, h * 128 : (h + 1) * 128], approx=True
                )
                cover[here, pl.ds(base + h * 128, 128)] = c.astype(jnp.bfloat16)
        total[...] += lax.dot_general(
            cover[:, pl.ds(base, columns)],
            estimate[:, pl.ds(base, columns)],
            NT,
            preferred_element_type=jnp.float32,
        )
        return carry

    lax.fori_loop(0, rows, row, 0)
    for s in range(GROUP):
        slot = step * GROUP + s
        value = jnp.transpose(total[s * antennas : (s + 1) * antennas, :])
        block = meta[slot]
        partial[block] = jnp.where(slot < meta[slots], partial[block] + value, partial[block])


def fill_weights(meta, settings, shares, weights):
    slots, antennas, maps = meta.shape[0] - 3, settings.shape[2], shares.shape[1]

    def pieces(x):
        high = x.astype(jnp.bfloat16)
        return high, x - high.astype(jnp.float32)

    first = lax.broadcasted_iota(jnp.int32, (16, antennas), 0)
    for s in range(slots):
        here = slice(s * antennas, (s + 1) * antennas)
        block = meta[s]
        live = s < meta[slots]
        high, rest = pieces(jnp.where(live, shares[block], 0.0))
        weights[0:maps, here] = high
        weights[maps : 2 * maps, here] = rest.astype(jnp.bfloat16)
        gain = jnp.where(live, jnp.broadcast_to(settings[block][3:4, :], (16, antennas)), 0.0)
        g0, rest = pieces(gain)
        g1, rest = pieces(rest)
        f0, f1, f2 = g0.astype(jnp.float32), g1.astype(jnp.float32), rest
        rows = jnp.where(first == 0, f0, jnp.where(first == 1, f1, jnp.where(first == 2, f2, 0.0)))
        weights[2 * maps : 2 * maps + 16, here] = rows.astype(jnp.bfloat16)


def updated(weights, cover, estimate):
    maps = estimate.shape[0]
    sums = jnp.dot(weights[...], cover[...], preferred_element_type=jnp.float32)
    sens = jnp.sum(sums[2 * maps :, :], axis=0, keepdims=True)
    return estimate[...] * (sums[:maps, :] + sums[maps : 2 * maps, :]) / sens


def middle_kernel(meta, settings, shares, cover, estimate, new, partial, weights, total):
    slots, antennas = meta.shape[0] - 3, settings.shape[2]
    step = pl.program_id(0)

    @pl.when(step == 0)
    def _():
        partial[...] = jnp.zeros_like(partial)
        total[...] = jnp.zeros_like(total)
        fill_weights(meta, settings, shares, weights)

    value = updated(weights, cover, estimate)
    new[...] = value
    narrow = value.astype(jnp.bfloat16)
    depth = GROUP * antennas
    for g in range(slots // GROUP):
        here = slice(g * depth, (g + 1) * depth)
        total[here, :] += lax.dot_general(
            cover[here, :], narrow, NT, preferred_element_type=jnp.float32
        )

    @pl.when(step == pl.num_programs(0) - 1)
    def _():
        for s in range(slots):
            value = jnp.transpose(total[s * antennas : (s + 1) * antennas, :])
            block = meta[s]
            partial[block] = jnp.where(s < meta[slots], partial[block] + value, partial[block])


def last_kernel(meta, settings, shares, cover, estimate, new, weights):
    @pl.when(pl.program_id(0) == 0)
    def _():
        fill_weights(meta, settings, shares, weights)

    new[...] = updated(weights, cover, estimate)


def whole(shape):
    return pl.BlockSpec(shape, lambda i, meta: (0,) * len(shape))


def shards(initial_estimate0, clutter, counts, antenna_settings, tile_block_list, tile_block_count):
    maps, rows, columns = initial_estimate0.shape
    n_pixels = rows * columns
    antennas = antenna_settings.shape[2]
    slots = tile_block_list.shape[2]
    n_blocks = lax.axis_size(("row", "col")) * counts.shape[0]
    depth = GROUP * antennas
    meta = jnp.concatenate(
        [
            tile_block_list.reshape(slots),
            tile_block_count.reshape(1),
            (lax.axis_index("row") * rows).astype(jnp.int32).reshape(1),
            (lax.axis_index("col") * columns).astype(jnp.int32).reshape(1),
        ]
    )
    estimate = initial_estimate0.reshape(maps, n_pixels)
    settings = lax.all_gather(
        jnp.pad(antenna_settings, ((0, 0), (0, 3), (0, 0))), ("row", "col"), axis=0, tiled=True
    )
    params = pltpu.CompilerParams(vmem_limit_bytes=VMEM, dimension_semantics=("arbitrary",))
    partial_shape = jax.ShapeDtypeStruct((n_blocks, maps, antennas), jnp.float32)
    cover, partial = pl.pallas_call(
        cover_kernel,
        out_shape=(
            jax.ShapeDtypeStruct((slots * antennas, n_pixels), jnp.bfloat16),
            partial_shape,
        ),
        grid_spec=pltpu.PrefetchScalarGridSpec(
            num_scalar_prefetch=1,
            grid=(slots // GROUP,),
            in_specs=[
                whole(settings.shape),
                whole((rows, 1, columns)),
                whole((maps, n_pixels)),
            ],
            out_specs=[
                pl.BlockSpec((depth, n_pixels), lambda i, meta: (i, 0)),
                whole(partial_shape.shape),
            ],
            scratch_shapes=[
                pltpu.VMEM((depth, columns), jnp.float32),
                pltpu.VMEM((depth, 128), jnp.float32),
                pltpu.VMEM((depth, 128), jnp.float32),
                pltpu.VMEM((depth, 128), jnp.float32),
                pltpu.VMEM((depth, maps), jnp.float32),
            ],
        ),
        compiler_params=params,
        name="cover_first",
    )(meta, settings, clutter.reshape(rows, 1, columns), estimate.astype(jnp.bfloat16))

    def share(partial):
        projected = lax.psum_scatter(partial, ("row", "col"), scatter_dimension=0, tiled=True)
        return lax.all_gather(
            counts.astype(jnp.float32) / projected, ("row", "col"), axis=0, tiled=True
        )

    pixel_spec = pl.BlockSpec((maps, CHUNK), lambda i, meta: (0, i))
    estimate_shape = jax.ShapeDtypeStruct((maps, n_pixels), jnp.float32)
    in_specs = [
        whole(settings.shape),
        whole(partial_shape.shape),
        pl.BlockSpec((slots * antennas, CHUNK), lambda i, meta: (0, i)),
        pixel_spec,
    ]
    weights = pltpu.VMEM((2 * maps + 16, slots * antennas), jnp.bfloat16)
    for sweep in range(ITERS - 1):
        estimate, partial = pl.pallas_call(
            middle_kernel,
            out_shape=(estimate_shape, partial_shape),
            grid_spec=pltpu.PrefetchScalarGridSpec(
                num_scalar_prefetch=1,
                grid=(n_pixels // CHUNK,),
                in_specs=in_specs,
                out_specs=[pixel_spec, whole(partial_shape.shape)],
                scratch_shapes=[weights, pltpu.VMEM((slots * antennas, maps), jnp.float32)],
            ),
            compiler_params=params,
            name="update_project",
        )(meta, settings, share(partial), cover, estimate)
    estimate = pl.pallas_call(
        last_kernel,
        out_shape=estimate_shape,
        grid_spec=pltpu.PrefetchScalarGridSpec(
            num_scalar_prefetch=1,
            grid=(n_pixels // CHUNK,),
            in_specs=in_specs,
            out_specs=pixel_spec,
            scratch_shapes=[weights],
        ),
        compiler_params=params,
        name="update_last",
    )(meta, settings, share(partial), cover, estimate)
    return estimate.reshape(maps, rows, columns)


def solution(mesh):
    in_specs = (
        P(None, "row", "col"),
        P("row", "col"),
        P(("row", "col"), None, None),
        P(("row", "col"), None, None),
        P("row", "col", None),
        P("row", "col"),
    )
    out_specs = P(None, "row", "col")
    return jax.shard_map(shards, mesh=mesh, in_specs=in_specs, out_specs=out_specs, check_vma=False)
```

```python
import functools

import jax
import jax.numpy as jnp
from jax import lax
from jax.experimental import pallas as pl
from jax.experimental.pallas import tpu as pltpu
from jax.sharding import PartitionSpec as P

ITERS = 2
GROUP = 4
CHUNK = 512
LOG2E = 1.4426950408889634
NT = (((1,), (1,)), ((), ()))
VMEM = 50 << 20
MESH = pl.DeviceIdType.MESH
PARTS = 3


def place(n_row, n_col):
    row, col = lax.axis_index("row"), lax.axis_index("col")
    rh, rl, ch, cl = row // 2, row % 2, col // 2, col % 2
    far_col, far_row = n_col // 2, n_row // 2
    ch_peers = [(ch + k) % far_col for k in range(1, far_col)]
    rh_peers = [(rh + k) % far_row for k in range(1, far_row)]
    partners = [
        [(row, col + 1 - 2 * cl)],
        [(row, p * 2 + cl) for p in ch_peers],
        [(row + 1 - 2 * rl, col)],
        [(p * 2 + rl, col) for p in rh_peers],
    ]
    return (rh, rl, ch, cl), ch_peers, rh_peers, partners


def greet(partners):
    barrier = pltpu.get_barrier_semaphore()
    everyone = [d for step in partners for d in step]
    for device in everyone:
        pl.semaphore_signal(barrier, inc=1, device_id=device, device_id_type=MESH)
    pl.semaphore_wait(barrier, len(everyone))


def launch(pairs, partners, send, recv, first):
    copies = []
    for k, ((source, target), device) in enumerate(zip(pairs, partners)):
        copy = pltpu.make_async_remote_copy(
            src_ref=source,
            dst_ref=target,
            send_sem=send.at[first + k],
            recv_sem=recv.at[first + k],
            device_id=device,
            device_id_type=MESH,
        )
        copy.start()
        copies.append(copy)
    return copies


def spread(out, digits, partners, cuts, send, recv, first):
    rh, rl, ch, cl = digits
    started = []
    before = None
    for step in (3, 2, 1, 0):
        current = []
        for q, cut in enumerate(cuts):
            if before is not None:
                for copy in before[q]:
                    copy.wait_recv()
            view = (
                out.at[:, :, :, cl, cut],
                out.at[:, :, ch, cl, cut],
                out.at[:, rl, ch, cl, cut],
                out.at[rh, rl, ch, cl, cut],
            )[step]
            pairs = [(view, view)] * len(partners[step])
            current.append(launch(pairs, partners[step], send, recv, first))
            first += len(pairs)
            started += current[-1]
        before = current
    for group in before:
        for copy in group:
            copy.wait_recv()
    for copy in started:
        copy.wait_send()


def gather_kernel(n_row, n_col, mine, out, send, recv):
    digits, _, _, partners = place(n_row, n_col)
    rh, rl, ch, cl = digits
    greet(partners)
    out[rh, rl, ch, cl] = mine[0]
    spread(out, digits, partners, [slice(0, mine.shape[1])], send, recv, 0)


def share_kernel(
    n_row, n_col, partial, counts, out, in0, in1, in2, in3, sum0, sum1, sum2, send, recv
):
    digits, ch_peers, rh_peers, partners = place(n_row, n_col)
    rh, rl, ch, cl = digits
    maps = counts.shape[1]
    piece = maps // PARTS
    cuts = [slice(q * piece, (q + 1) * piece) for q in range(PARTS)]
    greet(partners)
    first, started, before = 0, [], None
    for step in range(5):
        current = []
        for q, cut in enumerate(cuts):
            if before is not None:
                for copy in before[q]:
                    copy.wait_recv()
            if step == 0:
                pairs = [(partial.at[:, :, :, 1 - cl, cut], in0.at[:, :, :, cut])]
            elif step == 1:
                sum0[:, :, :, cut] = partial[:, :, :, cl, cut] + in0[:, :, :, cut]
                pairs = [
                    (sum0.at[:, :, p, cut], in1.at[k, :, :, cut]) for k, p in enumerate(ch_peers)
                ]
            elif step == 2:
                value = sum0[:, :, ch, cut]
                for k in range(len(ch_peers)):
                    value = value + in1[k, :, :, cut]
                sum1[:, :, cut] = value
                pairs = [(sum1.at[:, 1 - rl, cut], in2.at[:, cut])]
            elif step == 3:
                sum2[:, cut] = sum1[:, rl, cut] + in2[:, cut]
                pairs = [(sum2.at[p, cut], in3.at[k, cut]) for k, p in enumerate(rh_peers)]
            else:
                value = sum2[rh, cut]
                for k in range(len(rh_peers)):
                    value = value + in3[k, cut]
                out[rh, rl, ch, cl, cut] = counts[0, cut].astype(jnp.float32) / value
                continue
            current.append(launch(pairs, partners[step], send, recv, first))
            first += len(pairs)
            started += current[-1]
        before = current
    spread(out, digits, partners, cuts, send, recv, first)
    for copy in started:
        copy.wait_send()


def exchange(kernel, n_row, n_col, operands, block, scratch, copies, number, name):
    grid = (n_row // 2, 2, n_col // 2, 2)
    out = pl.pallas_call(
        functools.partial(kernel, n_row, n_col),
        out_shape=jax.ShapeDtypeStruct(grid + block, jnp.float32),
        in_specs=[pl.BlockSpec(memory_space=pltpu.VMEM)] * len(operands),
        out_specs=pl.BlockSpec(memory_space=pltpu.VMEM),
        scratch_shapes=[pltpu.VMEM(shape + block, jnp.float32) for shape in scratch]
        + [pltpu.SemaphoreType.DMA((copies,)), pltpu.SemaphoreType.DMA((copies,))],
        compiler_params=pltpu.CompilerParams(
            collective_id=number, has_side_effects=True, vmem_limit_bytes=VMEM
        ),
        name=name,
    )(*operands)
    return out.reshape((n_row * n_col,) + block)


def cover_kernel(
    meta, settings, clutter, estimate, cover, partial, column_term, slope, shift, inverse, total
):
    slots, rows, columns = meta.shape[0] - 3, clutter.shape[0], clutter.shape[2]
    antennas = settings.shape[2]
    step = pl.program_id(0)
    wide = (antennas, 128)

    @pl.when(step == 0)
    def _():
        partial[...] = jnp.zeros_like(partial)

    row_start = meta[slots + 1].astype(jnp.float32) + 0.5
    column_start = meta[slots + 2].astype(jnp.float32) + 0.5
    lanes = lax.broadcasted_iota(jnp.int32, wide, 1).astype(jnp.float32)
    for s in range(GROUP):
        here = slice(s * antennas, (s + 1) * antennas)
        record = jnp.transpose(settings[meta[step * GROUP + s]])
        inv = jnp.broadcast_to(1.0 / record[:, 2:3], wide)
        inverse[here, :] = inv
        shift[here, :] = (row_start - jnp.broadcast_to(record[:, 0:1], wide)) * inv
        slope[here, :] = jnp.broadcast_to(record[:, 4:5] * (-LOG2E), wide)
        position = jnp.broadcast_to(record[:, 1:2], wide)
        for h in range(columns // 128):
            d = (lanes + (column_start + h * 128.0) - position) * inv
            column_term[here, h * 128 : (h + 1) * 128] = 1.0 + d * d
    total[...] = jnp.zeros_like(total)

    def row(i, carry):
        base = pl.multiple_of(i * columns, columns)
        offset = i.astype(jnp.float32)
        for s in range(GROUP):
            here = slice(s * antennas, (s + 1) * antennas)
            d = shift[here, :] + offset * inverse[here, :]
            dd = d * d
            k = slope[here, :]
            for h in range(columns // 128):
                loss = clutter[i, :, h * 128 : (h + 1) * 128]
                c = jnp.exp2(k * loss) * pl.reciprocal(
                    dd + column_term[here, h * 128 : (h + 1) * 128], approx=True
                )
                cover[here, pl.ds(base + h * 128, 128)] = c.astype(jnp.bfloat16)
        total[...] += lax.dot_general(
            cover[:, pl.ds(base, columns)],
            estimate[:, pl.ds(base, columns)],
            NT,
            preferred_element_type=jnp.float32,
        )
        return carry

    lax.fori_loop(0, rows, row, 0)
    for s in range(GROUP):
        slot = step * GROUP + s
        value = jnp.transpose(total[s * antennas : (s + 1) * antennas, :])
        block = meta[slot]
        partial[block] = jnp.where(slot < meta[slots], partial[block] + value, partial[block])


def fill_weights(meta, settings, shares, weights):
    slots, antennas, maps = meta.shape[0] - 3, settings.shape[2], shares.shape[1]

    def pieces(x):
        high = x.astype(jnp.bfloat16)
        return high, x - high.astype(jnp.float32)

    first = lax.broadcasted_iota(jnp.int32, (16, antennas), 0)
    for s in range(slots):
        here = slice(s * antennas, (s + 1) * antennas)
        block = meta[s]
        live = s < meta[slots]
        high, rest = pieces(jnp.where(live, shares[block], 0.0))
        weights[0:maps, here] = high
        weights[maps : 2 * maps, here] = rest.astype(jnp.bfloat16)
        gain = jnp.where(live, jnp.broadcast_to(settings[block][3:4, :], (16, antennas)), 0.0)
        g0, rest = pieces(gain)
        g1, rest = pieces(rest)
        f0, f1, f2 = g0.astype(jnp.float32), g1.astype(jnp.float32), rest
        rows = jnp.where(first == 0, f0, jnp.where(first == 1, f1, jnp.where(first == 2, f2, 0.0)))
        weights[2 * maps : 2 * maps + 16, here] = rows.astype(jnp.bfloat16)


def updated(weights, cover, estimate):
    maps = estimate.shape[0]
    sums = jnp.dot(weights[...], cover[...], preferred_element_type=jnp.float32)
    sens = jnp.sum(sums[2 * maps :, :], axis=0, keepdims=True)
    return estimate[...] * (sums[:maps, :] + sums[maps : 2 * maps, :]) / sens


def middle_kernel(meta, settings, shares, cover, estimate, new, partial, weights, total):
    slots, antennas = meta.shape[0] - 3, settings.shape[2]
    step = pl.program_id(0)

    @pl.when(step == 0)
    def _():
        partial[...] = jnp.zeros_like(partial)
        total[...] = jnp.zeros_like(total)
        fill_weights(meta, settings, shares, weights)

    value = updated(weights, cover, estimate)
    new[...] = value
    narrow = value.astype(jnp.bfloat16)
    depth = GROUP * antennas
    for g in range(slots // GROUP):
        here = slice(g * depth, (g + 1) * depth)
        total[here, :] += lax.dot_general(
            cover[here, :], narrow, NT, preferred_element_type=jnp.float32
        )

    @pl.when(step == pl.num_programs(0) - 1)
    def _():
        for s in range(slots):
            value = jnp.transpose(total[s * antennas : (s + 1) * antennas, :])
            block = meta[s]
            partial[block] = jnp.where(s < meta[slots], partial[block] + value, partial[block])


def last_kernel(meta, settings, shares, cover, estimate, new, weights):
    @pl.when(pl.program_id(0) == 0)
    def _():
        fill_weights(meta, settings, shares, weights)

    new[...] = updated(weights, cover, estimate)


def whole(shape):
    return pl.BlockSpec(shape, lambda i, meta: (0,) * len(shape))


def shards(initial_estimate0, clutter, counts, antenna_settings, tile_block_list, tile_block_count):
    maps, rows, columns = initial_estimate0.shape
    n_pixels = rows * columns
    antennas = antenna_settings.shape[2]
    slots = tile_block_list.shape[2]
    n_blocks = lax.axis_size(("row", "col")) * counts.shape[0]
    depth = GROUP * antennas
    meta = jnp.concatenate(
        [
            tile_block_list.reshape(slots),
            tile_block_count.reshape(1),
            (lax.axis_index("row") * rows).astype(jnp.int32).reshape(1),
            (lax.axis_index("col") * columns).astype(jnp.int32).reshape(1),
        ]
    )
    estimate = initial_estimate0.reshape(maps, n_pixels)
    n_row, n_col = lax.axis_size("row"), lax.axis_size("col")
    far_row, far_col = n_row // 2, n_col // 2
    settings = exchange(
        gather_kernel,
        n_row,
        n_col,
        (jnp.pad(antenna_settings, ((0, 0), (0, 3), (0, 0))),),
        (8, antennas),
        [],
        far_row + far_col,
        1,
        "gather_settings",
    )
    params = pltpu.CompilerParams(vmem_limit_bytes=VMEM, dimension_semantics=("arbitrary",))
    partial_shape = jax.ShapeDtypeStruct((n_blocks, maps, antennas), jnp.float32)
    cover, partial = pl.pallas_call(
        cover_kernel,
        out_shape=(
            jax.ShapeDtypeStruct((slots * antennas, n_pixels), jnp.bfloat16),
            partial_shape,
        ),
        grid_spec=pltpu.PrefetchScalarGridSpec(
            num_scalar_prefetch=1,
            grid=(slots // GROUP,),
            in_specs=[
                whole(settings.shape),
                whole((rows, 1, columns)),
                whole((maps, n_pixels)),
            ],
            out_specs=[
                pl.BlockSpec((depth, n_pixels), lambda i, meta: (i, 0)),
                whole(partial_shape.shape),
            ],
            scratch_shapes=[
                pltpu.VMEM((depth, columns), jnp.float32),
                pltpu.VMEM((depth, 128), jnp.float32),
                pltpu.VMEM((depth, 128), jnp.float32),
                pltpu.VMEM((depth, 128), jnp.float32),
                pltpu.VMEM((depth, maps), jnp.float32),
            ],
        ),
        compiler_params=params,
        name="cover_first",
    )(meta, settings, clutter.reshape(rows, 1, columns), estimate.astype(jnp.bfloat16))

    def share(partial):
        return exchange(
            share_kernel,
            n_row,
            n_col,
            (partial.reshape(far_row, 2, far_col, 2, maps, antennas), counts),
            (maps, antennas),
            [
                (far_row, 2, far_col),
                (far_col - 1, far_row, 2),
                (far_row,),
                (far_row - 1,),
                (far_row, 2, far_col),
                (far_row, 2),
                (far_row,),
            ],
            2 * PARTS * (far_row + far_col),
            2,
            "share_ratios",
        )

    pixel_spec = pl.BlockSpec((maps, CHUNK), lambda i, meta: (0, i))
    estimate_shape = jax.ShapeDtypeStruct((maps, n_pixels), jnp.float32)
    in_specs = [
        whole(settings.shape),
        whole(partial_shape.shape),
        pl.BlockSpec((slots * antennas, CHUNK), lambda i, meta: (0, i)),
        pixel_spec,
    ]
    weights = pltpu.VMEM((2 * maps + 16, slots * antennas), jnp.bfloat16)
    for sweep in range(ITERS - 1):
        estimate, partial = pl.pallas_call(
            middle_kernel,
            out_shape=(estimate_shape, partial_shape),
            grid_spec=pltpu.PrefetchScalarGridSpec(
                num_scalar_prefetch=1,
                grid=(n_pixels // CHUNK,),
                in_specs=in_specs,
                out_specs=[pixel_spec, whole(partial_shape.shape)],
                scratch_shapes=[weights, pltpu.VMEM((slots * antennas, maps), jnp.float32)],
            ),
            compiler_params=params,
            name="update_project",
        )(meta, settings, share(partial), cover, estimate)
    estimate = pl.pallas_call(
        last_kernel,
        out_shape=estimate_shape,
        grid_spec=pltpu.PrefetchScalarGridSpec(
            num_scalar_prefetch=1,
            grid=(n_pixels // CHUNK,),
            in_specs=in_specs,
            out_specs=pixel_spec,
            scratch_shapes=[weights],
        ),
        compiler_params=params,
        name="update_last",
    )(meta, settings, share(partial), cover, estimate)
    return estimate.reshape(maps, rows, columns)


def solution(mesh):
    in_specs = (
        P(None, "row", "col"),
        P("row", "col"),
        P(("row", "col"), None, None),
        P(("row", "col"), None, None),
        P("row", "col", None),
        P("row", "col"),
    )
    out_specs = P(None, "row", "col")
    return jax.shard_map(shards, mesh=mesh, in_specs=in_specs, out_specs=out_specs, check_vma=False)
```

```python
import functools

import jax
import jax.numpy as jnp
from jax import lax
from jax.experimental import pallas as pl
from jax.experimental.pallas import tpu as pltpu
from jax.sharding import PartitionSpec as P

ITERS = 2
GROUP = 4
CHUNK = 512
LOG2E = 1.4426950408889634
NT = (((1,), (1,)), ((), ()))
VMEM = 50 << 20
MESH = pl.DeviceIdType.MESH
PARTS = 3


def place(n_row, n_col):
    row, col = lax.axis_index("row"), lax.axis_index("col")
    rh, rl, ch, cl = row // 2, row % 2, col // 2, col % 2
    far_col, far_row = n_col // 2, n_row // 2
    ch_peers = [(ch + k) % far_col for k in range(1, far_col)]
    rh_peers = [(rh + k) % far_row for k in range(1, far_row)]
    partners = [
        [(row, col + 1 - 2 * cl)],
        [(row, p * 2 + cl) for p in ch_peers],
        [(row + 1 - 2 * rl, col)],
        [(p * 2 + rl, col) for p in rh_peers],
    ]
    return (rh, rl, ch, cl), ch_peers, rh_peers, partners


def greet(partners):
    barrier = pltpu.get_barrier_semaphore()
    everyone = [d for step in partners for d in step]
    for device in everyone:
        pl.semaphore_signal(barrier, inc=1, device_id=device, device_id_type=MESH)
    pl.semaphore_wait(barrier, len(everyone))


def launch(pairs, partners, send, recv, first):
    copies = []
    for k, ((source, target), device) in enumerate(zip(pairs, partners)):
        copy = pltpu.make_async_remote_copy(
            src_ref=source,
            dst_ref=target,
            send_sem=send.at[first + k],
            recv_sem=recv.at[first + k],
            device_id=device,
            device_id_type=MESH,
        )
        copy.start()
        copies.append(copy)
    return copies


def spread(out, digits, partners, cuts, send, recv, first):
    rh, rl, ch, cl = digits
    started = []
    before = None
    for step in (3, 2, 1, 0):
        current = []
        for q, cut in enumerate(cuts):
            if before is not None:
                for copy in before[q]:
                    copy.wait_recv()
            view = (
                out.at[:, :, :, cl, cut],
                out.at[:, :, ch, cl, cut],
                out.at[:, rl, ch, cl, cut],
                out.at[rh, rl, ch, cl, cut],
            )[step]
            pairs = [(view, view)] * len(partners[step])
            current.append(launch(pairs, partners[step], send, recv, first))
            first += len(pairs)
            started += current[-1]
        before = current
    for group in before:
        for copy in group:
            copy.wait_recv()
    for copy in started:
        copy.wait_send()


def gather_kernel(n_row, n_col, mine, out, send, recv):
    digits, _, _, partners = place(n_row, n_col)
    rh, rl, ch, cl = digits
    greet(partners)
    out[rh, rl, ch, cl] = mine[0]
    spread(out, digits, partners, [slice(0, mine.shape[1])], send, recv, 0)


def share_kernel(
    n_row, n_col, partial, counts, out, in0, in1, in2, in3, sum0, sum1, sum2, send, recv
):
    digits, ch_peers, rh_peers, partners = place(n_row, n_col)
    rh, rl, ch, cl = digits
    maps = counts.shape[1]
    piece = maps // PARTS
    cuts = [slice(q * piece, (q + 1) * piece) for q in range(PARTS)]
    greet(partners)
    first, started, before = 0, [], None
    for step in range(5):
        current = []
        for q, cut in enumerate(cuts):
            if before is not None:
                for copy in before[q]:
                    copy.wait_recv()
            if step == 0:
                pairs = [(partial.at[:, :, :, 1 - cl, cut], in0.at[:, :, :, cut])]
            elif step == 1:
                sum0[:, :, :, cut] = partial[:, :, :, cl, cut] + in0[:, :, :, cut]
                pairs = [
                    (sum0.at[:, :, p, cut], in1.at[k, :, :, cut]) for k, p in enumerate(ch_peers)
                ]
            elif step == 2:
                value = sum0[:, :, ch, cut]
                for k in range(len(ch_peers)):
                    value = value + in1[k, :, :, cut]
                sum1[:, :, cut] = value
                pairs = [(sum1.at[:, 1 - rl, cut], in2.at[:, cut])]
            elif step == 3:
                sum2[:, cut] = sum1[:, rl, cut] + in2[:, cut]
                pairs = [(sum2.at[p, cut], in3.at[k, cut]) for k, p in enumerate(rh_peers)]
            else:
                value = sum2[rh, cut]
                for k in range(len(rh_peers)):
                    value = value + in3[k, cut]
                out[rh, rl, ch, cl, cut] = counts[0, cut].astype(jnp.float32) / value
                continue
            current.append(launch(pairs, partners[step], send, recv, first))
            first += len(pairs)
            started += current[-1]
        before = current
    spread(out, digits, partners, cuts, send, recv, first)
    for copy in started:
        copy.wait_send()


def exchange(kernel, n_row, n_col, operands, block, scratch, copies, number, name):
    grid = (n_row // 2, 2, n_col // 2, 2)
    out = pl.pallas_call(
        functools.partial(kernel, n_row, n_col),
        out_shape=jax.ShapeDtypeStruct(grid + block, jnp.float32),
        in_specs=[pl.BlockSpec(memory_space=pltpu.VMEM)] * len(operands),
        out_specs=pl.BlockSpec(memory_space=pltpu.VMEM),
        scratch_shapes=[pltpu.VMEM(shape + block, jnp.float32) for shape in scratch]
        + [pltpu.SemaphoreType.DMA((copies,)), pltpu.SemaphoreType.DMA((copies,))],
        compiler_params=pltpu.CompilerParams(
            collective_id=number, has_side_effects=True, vmem_limit_bytes=VMEM
        ),
        name=name,
    )(*operands)
    return out.reshape((n_row * n_col,) + block)


def cover_kernel(
    meta, settings, clutter, estimate, cover, partial, column_term, slope, shift, inverse, total,
    turned,
):
    slots, rows, columns = meta.shape[0] - 3, clutter.shape[0], clutter.shape[2]
    antennas = settings.shape[2]
    step = pl.program_id(0)
    wide = (antennas, 128)

    @pl.when(step == 0)
    def _():
        partial[...] = jnp.zeros_like(partial)
        for i in range(rows):
            here = slice(i * columns, (i + 1) * columns)
            turned[here, :] = jnp.transpose(estimate[:, here]).astype(jnp.bfloat16)

    row_start = meta[slots + 1].astype(jnp.float32) + 0.5
    column_start = meta[slots + 2].astype(jnp.float32) + 0.5
    lanes = lax.broadcasted_iota(jnp.int32, wide, 1).astype(jnp.float32)
    for s in range(GROUP):
        here = slice(s * antennas, (s + 1) * antennas)
        record = jnp.transpose(settings[meta[step * GROUP + s]])
        inv = jnp.broadcast_to(1.0 / record[:, 2:3], wide)
        inverse[here, :] = inv
        shift[here, :] = (row_start - jnp.broadcast_to(record[:, 0:1], wide)) * inv
        slope[here, :] = jnp.broadcast_to(record[:, 4:5] * (-LOG2E), wide)
        position = jnp.broadcast_to(record[:, 1:2], wide)
        for h in range(columns // 128):
            d = (lanes + (column_start + h * 128.0) - position) * inv
            column_term[here, h * 128 : (h + 1) * 128] = 1.0 + d * d
    total[...] = jnp.zeros_like(total)

    def row(i, carry):
        base = pl.multiple_of(i * columns, columns)
        offset = i.astype(jnp.float32)
        blocks = []
        for s in range(GROUP):
            here = slice(s * antennas, (s + 1) * antennas)
            halves = []
            d = shift[here, :] + offset * inverse[here, :]
            dd = d * d
            k = slope[here, :]
            for h in range(columns // 128):
                loss = clutter[i, :, h * 128 : (h + 1) * 128]
                c = jnp.exp2(k * loss) * pl.reciprocal(
                    dd + column_term[here, h * 128 : (h + 1) * 128], approx=True
                )
                halves.append(c.astype(jnp.bfloat16))
            blocks.append(jnp.concatenate(halves, axis=1))
            cover[here, pl.ds(base, columns)] = blocks[-1]
        total[...] += jnp.dot(
            jnp.concatenate(blocks, axis=0),
            turned[pl.ds(base, columns), :],
            preferred_element_type=jnp.float32,
        )
        return carry

    lax.fori_loop(0, rows, row, 0, unroll=2)
    for s in range(GROUP):
        slot = step * GROUP + s
        value = jnp.transpose(total[s * antennas : (s + 1) * antennas, :])
        block = meta[slot]
        partial[block] = jnp.where(slot < meta[slots], partial[block] + value, partial[block])


def fill_weights(meta, settings, shares, weights):
    slots, antennas, maps = meta.shape[0] - 3, settings.shape[2], shares.shape[1]

    def pieces(x):
        high = x.astype(jnp.bfloat16)
        return high, x - high.astype(jnp.float32)

    first = lax.broadcasted_iota(jnp.int32, (16, antennas), 0)
    for s in range(slots):
        here = slice(s * antennas, (s + 1) * antennas)
        block = meta[s]
        live = s < meta[slots]
        high, rest = pieces(jnp.where(live, shares[block], 0.0))
        weights[0:maps, here] = high
        weights[maps : 2 * maps, here] = rest.astype(jnp.bfloat16)
        gain = jnp.where(live, jnp.broadcast_to(settings[block][3:4, :], (16, antennas)), 0.0)
        g0, rest = pieces(gain)
        g1, rest = pieces(rest)
        f0, f1, f2 = g0.astype(jnp.float32), g1.astype(jnp.float32), rest
        rows = jnp.where(first == 0, f0, jnp.where(first == 1, f1, jnp.where(first == 2, f2, 0.0)))
        weights[2 * maps : 2 * maps + 16, here] = rows.astype(jnp.bfloat16)


def updated(weights, cover, estimate):
    maps = estimate.shape[0]
    sums = jnp.dot(weights[...], cover[...], preferred_element_type=jnp.float32)
    sens = jnp.sum(sums[2 * maps :, :], axis=0, keepdims=True)
    return estimate[...] * (sums[:maps, :] + sums[maps : 2 * maps, :]) / sens


def middle_kernel(meta, settings, shares, cover, estimate, new, partial, weights, total):
    slots, antennas = meta.shape[0] - 3, settings.shape[2]
    step = pl.program_id(0)

    @pl.when(step == 0)
    def _():
        partial[...] = jnp.zeros_like(partial)
        total[...] = jnp.zeros_like(total)
        fill_weights(meta, settings, shares, weights)

    value = updated(weights, cover, estimate)
    new[...] = value
    narrow = value.astype(jnp.bfloat16)
    depth = GROUP * antennas
    for g in range(slots // GROUP):
        here = slice(g * depth, (g + 1) * depth)
        total[here, :] += lax.dot_general(
            cover[here, :], narrow, NT, preferred_element_type=jnp.float32
        )

    @pl.when(step == pl.num_programs(0) - 1)
    def _():
        for s in range(slots):
            value = jnp.transpose(total[s * antennas : (s + 1) * antennas, :])
            block = meta[s]
            partial[block] = jnp.where(s < meta[slots], partial[block] + value, partial[block])


def last_kernel(meta, settings, shares, cover, estimate, new, weights):
    @pl.when(pl.program_id(0) == 0)
    def _():
        fill_weights(meta, settings, shares, weights)

    new[...] = updated(weights, cover, estimate)


def whole(shape):
    return pl.BlockSpec(shape, lambda i, meta: (0,) * len(shape))


def shards(initial_estimate0, clutter, counts, antenna_settings, tile_block_list, tile_block_count):
    maps, rows, columns = initial_estimate0.shape
    n_pixels = rows * columns
    antennas = antenna_settings.shape[2]
    slots = tile_block_list.shape[2]
    n_blocks = lax.axis_size(("row", "col")) * counts.shape[0]
    depth = GROUP * antennas
    meta = jnp.concatenate(
        [
            tile_block_list.reshape(slots),
            tile_block_count.reshape(1),
            (lax.axis_index("row") * rows).astype(jnp.int32).reshape(1),
            (lax.axis_index("col") * columns).astype(jnp.int32).reshape(1),
        ]
    )
    estimate = initial_estimate0.reshape(maps, n_pixels)
    n_row, n_col = lax.axis_size("row"), lax.axis_size("col")
    far_row, far_col = n_row // 2, n_col // 2
    settings = exchange(
        gather_kernel,
        n_row,
        n_col,
        (jnp.pad(antenna_settings, ((0, 0), (0, 3), (0, 0))),),
        (8, antennas),
        [],
        far_row + far_col,
        1,
        "gather_settings",
    )
    params = pltpu.CompilerParams(vmem_limit_bytes=VMEM, dimension_semantics=("arbitrary",))
    partial_shape = jax.ShapeDtypeStruct((n_blocks, maps, antennas), jnp.float32)
    cover, partial = pl.pallas_call(
        cover_kernel,
        out_shape=(
            jax.ShapeDtypeStruct((slots * antennas, n_pixels), jnp.bfloat16),
            partial_shape,
        ),
        grid_spec=pltpu.PrefetchScalarGridSpec(
            num_scalar_prefetch=1,
            grid=(slots // GROUP,),
            in_specs=[
                whole(settings.shape),
                whole((rows, 1, columns)),
                whole((maps, n_pixels)),
            ],
            out_specs=[
                pl.BlockSpec((depth, n_pixels), lambda i, meta: (i, 0)),
                whole(partial_shape.shape),
            ],
            scratch_shapes=[
                pltpu.VMEM((depth, columns), jnp.float32),
                pltpu.VMEM((depth, 128), jnp.float32),
                pltpu.VMEM((depth, 128), jnp.float32),
                pltpu.VMEM((depth, 128), jnp.float32),
                pltpu.VMEM((depth, maps), jnp.float32),
                pltpu.VMEM((n_pixels, maps), jnp.bfloat16),
            ],
        ),
        compiler_params=params,
        name="cover_first",
    )(meta, settings, clutter.reshape(rows, 1, columns), estimate)

    def share(partial):
        return exchange(
            share_kernel,
            n_row,
            n_col,
            (partial.reshape(far_row, 2, far_col, 2, maps, antennas), counts),
            (maps, antennas),
            [
                (far_row, 2, far_col),
                (far_col - 1, far_row, 2),
                (far_row,),
                (far_row - 1,),
                (far_row, 2, far_col),
                (far_row, 2),
                (far_row,),
            ],
            2 * PARTS * (far_row + far_col),
            2,
            "share_ratios",
        )

    pixel_spec = pl.BlockSpec((maps, CHUNK), lambda i, meta: (0, i))
    estimate_shape = jax.ShapeDtypeStruct((maps, n_pixels), jnp.float32)
    in_specs = [
        whole(settings.shape),
        whole(partial_shape.shape),
        pl.BlockSpec((slots * antennas, CHUNK), lambda i, meta: (0, i)),
        pixel_spec,
    ]
    weights = pltpu.VMEM((2 * maps + 16, slots * antennas), jnp.bfloat16)
    for sweep in range(ITERS - 1):
        estimate, partial = pl.pallas_call(
            middle_kernel,
            out_shape=(estimate_shape, partial_shape),
            grid_spec=pltpu.PrefetchScalarGridSpec(
                num_scalar_prefetch=1,
                grid=(n_pixels // CHUNK,),
                in_specs=in_specs,
                out_specs=[pixel_spec, whole(partial_shape.shape)],
                scratch_shapes=[weights, pltpu.VMEM((slots * antennas, maps), jnp.float32)],
            ),
            compiler_params=params,
            name="update_project",
        )(meta, settings, share(partial), cover, estimate)
    estimate = pl.pallas_call(
        last_kernel,
        out_shape=estimate_shape,
        grid_spec=pltpu.PrefetchScalarGridSpec(
            num_scalar_prefetch=1,
            grid=(n_pixels // CHUNK,),
            in_specs=in_specs,
            out_specs=pixel_spec,
            scratch_shapes=[weights],
        ),
        compiler_params=params,
        name="update_last",
    )(meta, settings, share(partial), cover, estimate)
    return estimate.reshape(maps, rows, columns)


def solution(mesh):
    in_specs = (
        P(None, "row", "col"),
        P("row", "col"),
        P(("row", "col"), None, None),
        P(("row", "col"), None, None),
        P("row", "col", None),
        P("row", "col"),
    )
    out_specs = P(None, "row", "col")
    return jax.shard_map(shards, mesh=mesh, in_specs=in_specs, out_specs=out_specs, check_vma=False)
```

```python
import functools

import jax
import jax.numpy as jnp
from jax import lax
from jax.experimental import pallas as pl
from jax.experimental.pallas import tpu as pltpu
from jax.sharding import PartitionSpec as P

ITERS = 2
GROUP = 4
CHUNK = 1024
LOG2E = 1.4426950408889634
NT = (((1,), (1,)), ((), ()))
VMEM = 50 << 20
MESH = pl.DeviceIdType.MESH
PARTS = 3


def place(n_row, n_col):
    row, col = lax.axis_index("row"), lax.axis_index("col")
    rh, rl, ch, cl = row // 2, row % 2, col // 2, col % 2
    far_col, far_row = n_col // 2, n_row // 2
    ch_peers = [(ch + k) % far_col for k in range(1, far_col)]
    rh_peers = [(rh + k) % far_row for k in range(1, far_row)]
    partners = [
        [(row, col + 1 - 2 * cl)],
        [(row, p * 2 + cl) for p in ch_peers],
        [(row + 1 - 2 * rl, col)],
        [(p * 2 + rl, col) for p in rh_peers],
    ]
    return (rh, rl, ch, cl), ch_peers, rh_peers, partners


def greet(partners):
    barrier = pltpu.get_barrier_semaphore()
    everyone = [d for step in partners for d in step]
    for device in everyone:
        pl.semaphore_signal(barrier, inc=1, device_id=device, device_id_type=MESH)
    pl.semaphore_wait(barrier, len(everyone))


def launch(pairs, partners, send, recv, first):
    copies = []
    for k, ((source, target), device) in enumerate(zip(pairs, partners)):
        copy = pltpu.make_async_remote_copy(
            src_ref=source,
            dst_ref=target,
            send_sem=send.at[first + k],
            recv_sem=recv.at[first + k],
            device_id=device,
            device_id_type=MESH,
        )
        copy.start()
        copies.append(copy)
    return copies


def spread(out, digits, partners, cuts, send, recv, first):
    rh, rl, ch, cl = digits
    started = []
    before = None
    for step in (3, 2, 1, 0):
        current = []
        for q, cut in enumerate(cuts):
            if before is not None:
                for copy in before[q]:
                    copy.wait_recv()
            view = (
                out.at[:, :, :, cl, cut],
                out.at[:, :, ch, cl, cut],
                out.at[:, rl, ch, cl, cut],
                out.at[rh, rl, ch, cl, cut],
            )[step]
            pairs = [(view, view)] * len(partners[step])
            current.append(launch(pairs, partners[step], send, recv, first))
            first += len(pairs)
            started += current[-1]
        before = current
    for group in before:
        for copy in group:
            copy.wait_recv()
    for copy in started:
        copy.wait_send()


def gather_kernel(n_row, n_col, mine, out, send, recv):
    digits, _, _, partners = place(n_row, n_col)
    rh, rl, ch, cl = digits
    greet(partners)
    out[rh, rl, ch, cl] = mine[0]
    spread(out, digits, partners, [slice(0, mine.shape[1])], send, recv, 0)


def share_kernel(
    n_row, n_col, partial, counts, out, in0, in1, in2, in3, sum0, sum1, sum2, send, recv
):
    digits, ch_peers, rh_peers, partners = place(n_row, n_col)
    rh, rl, ch, cl = digits
    maps = counts.shape[1]
    piece = maps // PARTS
    cuts = [slice(q * piece, (q + 1) * piece) for q in range(PARTS)]
    greet(partners)
    first, started, before = 0, [], None
    for step in range(5):
        current = []
        for q, cut in enumerate(cuts):
            if before is not None:
                for copy in before[q]:
                    copy.wait_recv()
            if step == 0:
                pairs = [(partial.at[:, :, :, 1 - cl, cut], in0.at[:, :, :, cut])]
            elif step == 1:
                sum0[:, :, :, cut] = partial[:, :, :, cl, cut] + in0[:, :, :, cut]
                pairs = [
                    (sum0.at[:, :, p, cut], in1.at[k, :, :, cut]) for k, p in enumerate(ch_peers)
                ]
            elif step == 2:
                value = sum0[:, :, ch, cut]
                for k in range(len(ch_peers)):
                    value = value + in1[k, :, :, cut]
                sum1[:, :, cut] = value
                pairs = [(sum1.at[:, 1 - rl, cut], in2.at[:, cut])]
            elif step == 3:
                sum2[:, cut] = sum1[:, rl, cut] + in2[:, cut]
                pairs = [(sum2.at[p, cut], in3.at[k, cut]) for k, p in enumerate(rh_peers)]
            else:
                value = sum2[rh, cut]
                for k in range(len(rh_peers)):
                    value = value + in3[k, cut]
                out[rh, rl, ch, cl, cut] = counts[0, cut].astype(jnp.float32) / value
                continue
            current.append(launch(pairs, partners[step], send, recv, first))
            first += len(pairs)
            started += current[-1]
        before = current
    spread(out, digits, partners, cuts, send, recv, first)
    for copy in started:
        copy.wait_send()


def exchange(kernel, n_row, n_col, operands, block, scratch, copies, number, name):
    grid = (n_row // 2, 2, n_col // 2, 2)
    out = pl.pallas_call(
        functools.partial(kernel, n_row, n_col),
        out_shape=jax.ShapeDtypeStruct(grid + block, jnp.float32),
        in_specs=[pl.BlockSpec(memory_space=pltpu.VMEM)] * len(operands),
        out_specs=pl.BlockSpec(memory_space=pltpu.VMEM),
        scratch_shapes=[pltpu.VMEM(shape + block, jnp.float32) for shape in scratch]
        + [pltpu.SemaphoreType.DMA((copies,)), pltpu.SemaphoreType.DMA((copies,))],
        compiler_params=pltpu.CompilerParams(
            collective_id=number, has_side_effects=True, vmem_limit_bytes=VMEM
        ),
        name=name,
    )(*operands)
    return out.reshape((n_row * n_col,) + block)


def cover_kernel(
    meta, settings, clutter, estimate, cover, partial, column_term, slope, shift, inverse, total,
    turned,
):
    slots, rows, columns = meta.shape[0] - 3, clutter.shape[0], clutter.shape[2]
    antennas = settings.shape[2]
    step = pl.program_id(0)
    wide = (antennas, 128)

    @pl.when(step == 0)
    def _():
        partial[...] = jnp.zeros_like(partial)
        for i in range(rows):
            here = slice(i * columns, (i + 1) * columns)
            turned[here, :] = jnp.transpose(estimate[:, here]).astype(jnp.bfloat16)

    row_start = meta[slots + 1].astype(jnp.float32) + 0.5
    column_start = meta[slots + 2].astype(jnp.float32) + 0.5
    lanes = lax.broadcasted_iota(jnp.int32, wide, 1).astype(jnp.float32)
    for s in range(GROUP):
        here = slice(s * antennas, (s + 1) * antennas)
        record = jnp.transpose(settings[meta[step * GROUP + s]])
        inv = jnp.broadcast_to(1.0 / record[:, 2:3], wide)
        inverse[here, :] = inv
        shift[here, :] = (row_start - jnp.broadcast_to(record[:, 0:1], wide)) * inv
        slope[here, :] = jnp.broadcast_to(record[:, 4:5] * (-LOG2E), wide)
        position = jnp.broadcast_to(record[:, 1:2], wide)
        for h in range(columns // 128):
            d = (lanes + (column_start + h * 128.0) - position) * inv
            column_term[here, h * 128 : (h + 1) * 128] = 1.0 + d * d
    total[...] = jnp.zeros_like(total)

    def row(i, carry):
        base = pl.multiple_of(i * columns, columns)
        offset = i.astype(jnp.float32)
        blocks = []
        for s in range(GROUP):
            here = slice(s * antennas, (s + 1) * antennas)
            halves = []
            d = shift[here, :] + offset * inverse[here, :]
            dd = d * d
            k = slope[here, :]
            for h in range(columns // 128):
                loss = clutter[i, :, h * 128 : (h + 1) * 128]
                c = jnp.exp2(k * loss) * pl.reciprocal(
                    dd + column_term[here, h * 128 : (h + 1) * 128], approx=True
                )
                halves.append(c.astype(jnp.bfloat16))
            blocks.append(jnp.concatenate(halves, axis=1))
            cover[here, pl.ds(base, columns)] = blocks[-1]
        total[...] += jnp.dot(
            jnp.concatenate(blocks, axis=0),
            turned[pl.ds(base, columns), :],
            preferred_element_type=jnp.float32,
        )
        return carry

    lax.fori_loop(0, rows, row, 0, unroll=4)
    for s in range(GROUP):
        slot = step * GROUP + s
        value = jnp.transpose(total[s * antennas : (s + 1) * antennas, :])
        block = meta[slot]
        partial[block] = jnp.where(slot < meta[slots], partial[block] + value, partial[block])


def fill_weights(meta, settings, shares, weights):
    slots, antennas, maps = meta.shape[0] - 3, settings.shape[2], shares.shape[1]

    def pieces(x):
        high = x.astype(jnp.bfloat16)
        return high, x - high.astype(jnp.float32)

    first = lax.broadcasted_iota(jnp.int32, (16, antennas), 0)
    for s in range(slots):
        here = slice(s * antennas, (s + 1) * antennas)
        block = meta[s]
        live = s < meta[slots]
        high, rest = pieces(jnp.where(live, shares[block], 0.0))
        weights[0:maps, here] = high
        weights[maps : 2 * maps, here] = rest.astype(jnp.bfloat16)
        gain = jnp.where(live, jnp.broadcast_to(settings[block][3:4, :], (16, antennas)), 0.0)
        g0, rest = pieces(gain)
        g1, rest = pieces(rest)
        f0, f1, f2 = g0.astype(jnp.float32), g1.astype(jnp.float32), rest
        rows = jnp.where(first == 0, f0, jnp.where(first == 1, f1, jnp.where(first == 2, f2, 0.0)))
        weights[2 * maps : 2 * maps + 16, here] = rows.astype(jnp.bfloat16)


def updated(weights, cover, estimate):
    maps = estimate.shape[0]
    sums = jnp.dot(weights[...], cover[...], preferred_element_type=jnp.float32)
    sens = jnp.sum(sums[2 * maps :, :], axis=0, keepdims=True)
    return estimate[...] * (sums[:maps, :] + sums[maps : 2 * maps, :]) / sens


def middle_kernel(meta, settings, shares, cover, estimate, new, partial, weights, total):
    slots, antennas = meta.shape[0] - 3, settings.shape[2]
    step = pl.program_id(0)

    @pl.when(step == 0)
    def _():
        partial[...] = jnp.zeros_like(partial)
        total[...] = jnp.zeros_like(total)
        fill_weights(meta, settings, shares, weights)

    value = updated(weights, cover, estimate)
    new[...] = value
    narrow = value.astype(jnp.bfloat16)
    depth = GROUP * antennas
    for g in range(slots // GROUP):
        here = slice(g * depth, (g + 1) * depth)
        total[here, :] += lax.dot_general(
            cover[here, :], narrow, NT, preferred_element_type=jnp.float32
        )

    @pl.when(step == pl.num_programs(0) - 1)
    def _():
        for s in range(slots):
            value = jnp.transpose(total[s * antennas : (s + 1) * antennas, :])
            block = meta[s]
            partial[block] = jnp.where(s < meta[slots], partial[block] + value, partial[block])


def last_kernel(meta, settings, shares, cover, estimate, new, weights):
    @pl.when(pl.program_id(0) == 0)
    def _():
        fill_weights(meta, settings, shares, weights)

    new[...] = updated(weights, cover, estimate)


def whole(shape):
    return pl.BlockSpec(shape, lambda i, meta: (0,) * len(shape))


def shards(initial_estimate0, clutter, counts, antenna_settings, tile_block_list, tile_block_count):
    maps, rows, columns = initial_estimate0.shape
    n_pixels = rows * columns
    antennas = antenna_settings.shape[2]
    slots = tile_block_list.shape[2]
    n_blocks = lax.axis_size(("row", "col")) * counts.shape[0]
    depth = GROUP * antennas
    meta = jnp.concatenate(
        [
            tile_block_list.reshape(slots),
            tile_block_count.reshape(1),
            (lax.axis_index("row") * rows).astype(jnp.int32).reshape(1),
            (lax.axis_index("col") * columns).astype(jnp.int32).reshape(1),
        ]
    )
    estimate = initial_estimate0.reshape(maps, n_pixels)
    n_row, n_col = lax.axis_size("row"), lax.axis_size("col")
    far_row, far_col = n_row // 2, n_col // 2
    settings = exchange(
        gather_kernel,
        n_row,
        n_col,
        (jnp.pad(antenna_settings, ((0, 0), (0, 3), (0, 0))),),
        (8, antennas),
        [],
        far_row + far_col,
        1,
        "gather_settings",
    )
    params = pltpu.CompilerParams(vmem_limit_bytes=VMEM, dimension_semantics=("arbitrary",))
    partial_shape = jax.ShapeDtypeStruct((n_blocks, maps, antennas), jnp.float32)
    cover, partial = pl.pallas_call(
        cover_kernel,
        out_shape=(
            jax.ShapeDtypeStruct((slots * antennas, n_pixels), jnp.bfloat16),
            partial_shape,
        ),
        grid_spec=pltpu.PrefetchScalarGridSpec(
            num_scalar_prefetch=1,
            grid=(slots // GROUP,),
            in_specs=[
                whole(settings.shape),
                whole((rows, 1, columns)),
                whole((maps, n_pixels)),
            ],
            out_specs=[
                pl.BlockSpec((depth, n_pixels), lambda i, meta: (i, 0)),
                whole(partial_shape.shape),
            ],
            scratch_shapes=[
                pltpu.VMEM((depth, columns), jnp.float32),
                pltpu.VMEM((depth, 128), jnp.float32),
                pltpu.VMEM((depth, 128), jnp.float32),
                pltpu.VMEM((depth, 128), jnp.float32),
                pltpu.VMEM((depth, maps), jnp.float32),
                pltpu.VMEM((n_pixels, maps), jnp.bfloat16),
            ],
        ),
        compiler_params=params,
        name="cover_first",
    )(meta, settings, clutter.reshape(rows, 1, columns), estimate)

    def share(partial):
        return exchange(
            share_kernel,
            n_row,
            n_col,
            (partial.reshape(far_row, 2, far_col, 2, maps, antennas), counts),
            (maps, antennas),
            [
                (far_row, 2, far_col),
                (far_col - 1, far_row, 2),
                (far_row,),
                (far_row - 1,),
                (far_row, 2, far_col),
                (far_row, 2),
                (far_row,),
            ],
            2 * PARTS * (far_row + far_col),
            2,
            "share_ratios",
        )

    pixel_spec = pl.BlockSpec((maps, CHUNK), lambda i, meta: (0, i))
    estimate_shape = jax.ShapeDtypeStruct((maps, n_pixels), jnp.float32)
    in_specs = [
        whole(settings.shape),
        whole(partial_shape.shape),
        pl.BlockSpec((slots * antennas, CHUNK), lambda i, meta: (0, i)),
        pixel_spec,
    ]
    weights = pltpu.VMEM((2 * maps + 16, slots * antennas), jnp.bfloat16)
    for sweep in range(ITERS - 1):
        estimate, partial = pl.pallas_call(
            middle_kernel,
            out_shape=(estimate_shape, partial_shape),
            grid_spec=pltpu.PrefetchScalarGridSpec(
                num_scalar_prefetch=1,
                grid=(n_pixels // CHUNK,),
                in_specs=in_specs,
                out_specs=[pixel_spec, whole(partial_shape.shape)],
                scratch_shapes=[weights, pltpu.VMEM((slots * antennas, maps), jnp.float32)],
            ),
            compiler_params=params,
            name="update_project",
        )(meta, settings, share(partial), cover, estimate)
    estimate = pl.pallas_call(
        last_kernel,
        out_shape=estimate_shape,
        grid_spec=pltpu.PrefetchScalarGridSpec(
            num_scalar_prefetch=1,
            grid=(n_pixels // CHUNK,),
            in_specs=in_specs,
            out_specs=pixel_spec,
            scratch_shapes=[weights],
        ),
        compiler_params=params,
        name="update_last",
    )(meta, settings, share(partial), cover, estimate)
    return estimate.reshape(maps, rows, columns)


def solution(mesh):
    in_specs = (
        P(None, "row", "col"),
        P("row", "col"),
        P(("row", "col"), None, None),
        P(("row", "col"), None, None),
        P("row", "col", None),
        P("row", "col"),
    )
    out_specs = P(None, "row", "col")
    return jax.shard_map(shards, mesh=mesh, in_specs=in_specs, out_specs=out_specs, check_vma=False)
```
